32 devices in a mesh: segment: 2 (over x), dev: 16 (over z, y, core).
Axes of the slice: x: 2, y: 2, z: 4, core: 2. Of those that a mesh axis runs over, the one named last changes fastest.
Arguments:
- queries: bfloat16 [32, 8192], P(('segment', 'dev')), may hold values from -64 to 64
- page_ids: int32 [32, 4, 32], P(('segment', 'dev')), may hold values from 0 to 255, as said below
- key_pages: bfloat16 [512, 64, 128], P(('segment', 'dev')), may hold values from -6 to 6
- value_pages: bfloat16 [512, 64, 128], P(('segment', 'dev')), may hold values from -6 to 6
- out_weight: bfloat16 [16384, 16384], P(('segment', 'dev')), may hold values from -0.1875 to 0.1875
Outputs:
- block_out: bfloat16 [32, 16384], P(('segment', 'dev'))
The draws below stay inside these ranges and needn't reach their ends.
Inputs may be any that keep to these rules, and one draw needn't show every extreme that they name: `page_ids`: within the rows of one device (aligned blocks of 1 row), at most 16 of the entries name pages of one device (id // 16); in every section one such device, the same for all of its row blocks, is named exactly 16 times from each block. The 32 ids of one row and key head are distinct.
All inputs are finite; a program needn't handle non-finite values.
Results may differ from the reference program's by a relative error of at most 0.006.
Values may be sent and summed in bfloat16 or wider, within the bound.
A program may use at most 64 MiB of HBM per device.

```python
import math
import jax
import jax.numpy as jnp
from jax import lax

D = 16384
HQ = 64
KVH = 4
HD = 128
PAGE = 64
SEL = 32
ROWS_DEV = 1
PAGES_DEV = 16
GROUP = 16
R_SEC = 16
ROWS = 32
PAGES = 256
N_SEGMENT = 2
N_DEV = 16


def draw_queries(key, part):
    array_shape = (ROWS, HQ * HD)
    drawn = jnp.clip(2.0 * jax.random.normal(jax.random.fold_in(key, 12), array_shape, jnp.float32), -8.0, 8.0)
    return drawn.astype(jnp.bfloat16)


def draw_key_pages(key, part):
    array_shape = (N_SEGMENT * PAGES, PAGE, HD)
    drawn = jnp.clip(jax.random.normal(jax.random.fold_in(key, 22), array_shape, jnp.float32), -6.0, 6.0)
    return drawn.astype(jnp.bfloat16)


def draw_page_ids(key, part):
    per_block = ROWS_DEV * KVH * SEL
    blocks = ROWS // ROWS_DEV
    capacity = 2 * per_block // N_DEV
    position = jnp.arange(per_block, dtype=jnp.int32)
    hot_section = jax.random.randint(jax.random.fold_in(key, 31), (blocks // N_DEV,), 0, N_DEV, dtype=jnp.int32)
    hot_block = jnp.repeat(hot_section, N_DEV)[:, None]
    others = (hot_block + 1 + (position[None, :] - capacity) % (N_DEV - 1)) % N_DEV
    owners = jnp.where(position[None, :] < capacity, hot_block, others)
    block_keys = jax.random.split(jax.random.fold_in(key, 32), blocks)
    orders = jax.vmap(lambda one_key: jax.random.permutation(one_key, per_block))(block_keys)
    owners = jnp.take_along_axis(owners, orders.astype(jnp.int32), axis=1)
    owners = owners.reshape(ROWS * KVH, SEL)
    chosen_index = jnp.arange(SEL, dtype=jnp.int32)
    matches = (owners[:, :, None] == owners[:, None, :]) & (chosen_index[None, None, :] < chosen_index[None, :, None])
    rank_ids = jnp.sum(matches.astype(jnp.int32), axis=2)
    offsets = jax.random.randint(jax.random.fold_in(key, 33), (ROWS * KVH, 1), 0, PAGES_DEV, dtype=jnp.int32)
    slot_ids = (offsets + rank_ids) % PAGES_DEV
    return (owners * PAGES_DEV + slot_ids).reshape(ROWS, KVH, SEL).astype(jnp.int32)


def steps_of(key, dims, cuts, low, top_value):
    loudness = 1.0
    for dim, parts in cuts:
        draws = jax.random.uniform(jax.random.fold_in(jax.random.fold_in(key, 6), dim), (parts,), jnp.float32, low / len(cuts), top_value / len(cuts))
        loudness = loudness * jnp.repeat(jnp.exp(draws), dims[dim] // parts).reshape((-1,) + (1,) * (len(dims) - 1 - dim))
    return loudness


def bell_draw(rng, extent, scale, bound, cuts=(), kind=jnp.bfloat16):
    array = scale * jax.random.normal(rng, extent, jnp.float32)
    if cuts:
        array = array * steps_of(rng, extent, cuts, -0.22, 0.18)
    return jnp.clip(array, -bound, bound).astype(kind)


def setup_inputs(seed: int = 0) -> dict:
    arg_keys = jax.random.split(jax.random.key(seed), 6)
    return {
        "queries": draw_queries(jax.random.fold_in(arg_keys[5], 71), 0),
        "page_ids": draw_page_ids(jax.random.fold_in(arg_keys[5], 71), 0),
        "key_pages": draw_key_pages(jax.random.fold_in(arg_keys[5], 71), 0),
        "value_pages": bell_draw(arg_keys[3], (N_SEGMENT * PAGES, PAGE, HD), 1.0, 6.0, ((0, 32),)),
        "out_weight": bell_draw(arg_keys[4], (N_SEGMENT * HQ * HD, D), (HQ * HD // 8) ** -0.5, 0.1875, ((0, 32),)),
    }


def section_rows(query_rows, id_rows, key_pool, value_pool):
    score_scale = 1.0 / math.sqrt(HD)

    def one_row(row_pair):
        query_row, id_row = row_pair
        query_heads = query_row.reshape(KVH, GROUP, HD).astype(jnp.float32)
        page_keys = key_pool[id_row].astype(jnp.float32)
        page_values = value_pool[id_row].astype(jnp.float32)
        scores = jnp.einsum('kgd,kptd->kgpt', query_heads, page_keys) * score_scale
        page_max = lax.optimization_barrier(jnp.max(scores, axis=-1))
        rounded = jnp.exp(scores - page_max[..., None]).astype(jnp.bfloat16)
        weights = lax.optimization_barrier(rounded).astype(jnp.float32)
        weight_sum = lax.optimization_barrier(jnp.sum(weights, axis=-1))
        partial_value = jnp.einsum('kgpt,kptd->kgpd', weights, page_values)
        highest = lax.optimization_barrier(jnp.max(page_max, axis=-1, keepdims=True))
        factor = jnp.exp(page_max - highest)
        numerator = lax.optimization_barrier(jnp.sum(factor[..., None] * partial_value, axis=2))
        denominator = lax.optimization_barrier(jnp.sum(factor * weight_sum, axis=2))
        attended = numerator / denominator[..., None]
        return attended.reshape(-1).astype(jnp.bfloat16)
    return lax.map(one_row, (query_rows, id_rows))

def reference(queries, page_ids, key_pages, value_pages, out_weight):
    head_width = HQ * HD
    outputs = []
    for section in range(N_SEGMENT):
        row_lo = section * R_SEC
        page_lo = section * PAGES
        attended = section_rows(queries[row_lo:row_lo + R_SEC], page_ids[row_lo:row_lo + R_SEC], key_pages[page_lo:page_lo + PAGES], value_pages[page_lo:page_lo + PAGES])
        weight_rows = out_weight[section * head_width:(section + 1) * head_width]
        projected = jnp.dot(attended, weight_rows, preferred_element_type=jnp.float32).astype(jnp.bfloat16)
        outputs.append(projected)
    return jnp.roll(jnp.concatenate(outputs, axis=0), R_SEC, axis=0)
```

```python
import functools
import math

import jax
import jax.numpy as jnp
from jax import lax
from jax.experimental import pallas as pl
from jax.experimental.pallas import tpu as pltpu
from jax.sharding import PartitionSpec as P

MESH = pl.DeviceIdType.MESH
LANES = 128
CHUNKS = 4
BIG = float(2.0**100)


def kernel(dims, q_ref, ids_ref, key_ref, value_ref, weight_ref, out_ref,
           w_buf, k_buf, v_buf, page_hot, q_stage, q32, m_stage, q_buf, m_buf, q_aug, o_scr,
           p_send, p_recv, att, own_sum, c_send, c_recv, t_scr, f_send, f_recv,
           w_sem, kv_sem, kv_send, kv_recv, q_ssem, q_rsem, m_ssem, m_rsem, p_ssem, p_rsem,
           c_ssem, c_rsem, f_ssem, f_rsem):
    n, segments, kv_heads, chosen, pool, page, hd, group, width = dims
    half = n // 2
    hpd = kv_heads * group // n
    per_kv = group // 2
    tokens = pool * page
    span = 2 * pool
    cols = width // CHUNKS
    blocks = cols // LANES
    seg = lax.axis_index("segment")
    me = lax.axis_index("dev")
    core = lax.rem(me, 2)
    pair = me // 2
    mate = me + 1 - 2 * core
    slot = core * half + pair
    ahead = lax.rem(seg + 1, segments)
    behind = lax.rem(seg + segments - 1, segments)

    def weight_copy(k):
        return pltpu.make_async_copy(
            weight_ref.at[:, pl.ds(pl.multiple_of(k * cols, cols), cols)], w_buf.at[k], w_sem.at[k])

    barrier = pltpu.get_barrier_semaphore()

    @pl.loop(1, n)
    def _(k):
        pl.semaphore_signal(barrier, inc=1, device_id=(seg, lax.rem(me + k, n)), device_id_type=MESH)

    @pl.loop(0, half)
    def _(j):
        pl.semaphore_signal(barrier, inc=1, device_id=(behind, 2 * j + core), device_id_type=MESH)

    here = pl.ds(pl.multiple_of(core * tokens, tokens), tokens)
    key_local = pltpu.make_async_copy(key_ref, k_buf.at[here], kv_sem.at[0])
    value_local = pltpu.make_async_copy(value_ref, v_buf.at[here], kv_sem.at[1])
    key_local.start()
    value_local.start()

    @pl.loop(0, CHUNKS)
    def _(k):
        weight_copy(k).start()

    for c in range(2):
        for h in range(kv_heads):
            for u in range(per_kv // hpd):
                for i in range(hpd):
                    head = h * group + u * 2 * hpd + c * hpd + i
                    place = h * per_kv + u * hpd + i
                    q32[c, place:place + 1, :] = q_ref[0:1, head * hd:(head + 1) * hd].astype(jnp.float32)
    q_stage[...] = q32[...].astype(jnp.bfloat16)

    head_of_lane = lax.broadcasted_iota(jnp.int32, (kv_heads, LANES), 1) // span
    pick = (head_of_lane == lax.broadcasted_iota(jnp.int32, (kv_heads, LANES), 0)).astype(jnp.float32)
    ids = ids_ref[0].astype(jnp.float32)
    spread = lax.dot_general(ids, pick, (((0,), (0,)), ((), ())),
                             precision=lax.Precision.HIGHEST, preferred_element_type=jnp.float32)
    in_span = lax.rem(lax.broadcasted_iota(jnp.int32, (chosen, LANES), 1), span).astype(jnp.float32)
    offset = spread - in_span
    for j in range(half):
        hit = (jnp.abs(offset - float(j * span)) < 0.5).astype(jnp.float32)
        m_stage[j] = jnp.max(hit, axis=0, keepdims=True)

    q_buf[slot] = q_stage[core]
    m_buf[slot] = m_stage[pair]

    pl.semaphore_wait(barrier, n - 1 + half)

    def query_copy(k):
        peer = lax.rem(me + k, n)
        return pltpu.make_async_remote_copy(
            src_ref=q_stage.at[lax.rem(peer, 2)], dst_ref=q_buf.at[slot],
            send_sem=q_ssem.at[k], recv_sem=q_rsem.at[slot],
            device_id=(seg, peer), device_id_type=MESH)

    def mask_copy(k):
        peer = lax.rem(me + k, n)
        return pltpu.make_async_remote_copy(
            src_ref=m_stage.at[peer // 2], dst_ref=m_buf.at[slot],
            send_sem=m_ssem.at[k], recv_sem=m_rsem.at[slot],
            device_id=(seg, peer), device_id_type=MESH)

    @pl.loop(1, n)
    def _(k):
        query_copy(k).start()
        mask_copy(k).start()

    key_remote = pltpu.make_async_remote_copy(
        src_ref=key_ref, dst_ref=k_buf.at[here], send_sem=kv_send.at[0], recv_sem=kv_recv.at[0],
        device_id=(seg, mate), device_id_type=MESH)
    value_remote = pltpu.make_async_remote_copy(
        src_ref=value_ref, dst_ref=v_buf.at[here], send_sem=kv_send.at[1], recv_sem=kv_recv.at[1],
        device_id=(seg, mate), device_id_type=MESH)
    key_remote.start()
    value_remote.start()

    lane_page = lax.rem(lax.broadcasted_iota(jnp.int32, (2 * tokens, LANES), 1), span)
    token_page = lax.broadcasted_iota(jnp.int32, (2 * tokens, LANES), 0) // page
    page_hot[...] = jnp.where(lane_page == token_page, BIG, 0.0).astype(jnp.bfloat16)

    key_local.wait()
    value_local.wait()
    key_remote.wait()
    value_remote.wait()

    @pl.loop(1, n)
    def _(k):
        source = lax.rem(me + n - k, n)
        place = lax.rem(source, 2) * half + source // 2
        pltpu.make_async_copy(q_buf.at[place], q_buf.at[place], q_rsem.at[place]).wait()
        pltpu.make_async_copy(m_buf.at[place], m_buf.at[place], m_rsem.at[place]).wait()

    lane3 = lax.broadcasted_iota(jnp.int32, (n, 1, LANES), 2) // span
    absent = m_buf[...] - 1.0
    all_q = q_buf[...].astype(jnp.float32)
    for h in range(kv_heads):
        bias = jnp.where(lane3 == h, absent, 0.0)
        bias = jnp.broadcast_to(bias, (n, per_kv, LANES)).reshape(n * per_kv, LANES)
        q_aug[h, :, 0:hd] = all_q[:, h * per_kv:(h + 1) * per_kv, :].reshape(n * per_kv, hd).astype(jnp.bfloat16)
        q_aug[h, :, hd:hd + LANES] = bias.astype(jnp.bfloat16)

    def part_copy(j):
        return pltpu.make_async_remote_copy(
            src_ref=p_send.at[j], dst_ref=p_recv.at[pair],
            send_sem=p_ssem.at[j], recv_sem=p_rsem.at[pair],
            device_id=(seg, 2 * j + core), device_id_type=MESH)

    scale = math.log2(math.e) / math.sqrt(hd)
    lane = lax.broadcasted_iota(jnp.int32, (16, LANES), 1)
    units = per_kv // hpd

    @pl.loop(0, kv_heads)
    def _(h):
        keys = jnp.concatenate([k_buf[...], page_hot[...]], axis=1)
        values = jnp.concatenate([v_buf[...], jnp.ones((2 * tokens, LANES), jnp.bfloat16)], axis=1)
        for rb in range(n // 16):
            queries = q_aug[h, rb * 16 * per_kv:(rb + 1) * 16 * per_kv, :]
            scores = lax.dot_general(queries, keys, (((1,), (1,)), ((), ())),
                                     preferred_element_type=jnp.float32)
            top = jnp.max(scores, axis=1, keepdims=True) * scale
            weights = jnp.exp2(scores * scale - top).astype(jnp.bfloat16)
            sums = jnp.dot(weights, values, preferred_element_type=jnp.float32)
            o_scr[0] = sums[:, 0:hd] / sums[:, hd:]
            o_scr[1] = top + jnp.log2(sums[:, hd:])
            rows = slice(rb * 16, (rb + 1) * 16)
            for u in range(units):
                level = jnp.zeros((16, LANES), jnp.float32)
                for i in range(hpd):
                    index = u * hpd + i
                    value = o_scr[0, pl.ds(index, 16, stride=per_kv), :]
                    p_send[h * units + u, rows, i * hd:(i + 1) * hd] = value.astype(jnp.bfloat16)
                    level = jnp.where(lax.rem(lane, 32) == i, o_scr[1, pl.ds(index, 16, stride=per_kv), :], level)
                high = level.astype(jnp.bfloat16)
                rest = level - high.astype(jnp.float32)
                middle = rest.astype(jnp.bfloat16)
                low = rest - middle.astype(jnp.float32)
                packed = jnp.where(lane < 32, high.astype(jnp.float32),
                                   jnp.where(lane < 64, middle.astype(jnp.float32), low))
                p_send[h * units + u, rows, hpd * hd:hpd * hd + LANES] = packed.astype(jnp.bfloat16)
        for u in range(units):
            j = h * units + u

            @pl.when(j != pair)
            def _():
                part_copy(j).start()

            @pl.when(j == pair)
            def _():
                p_recv[pair] = p_send[j]

    @pl.loop(1, half)
    def _(k):
        source = lax.rem(pair + half - k, half)
        pltpu.make_async_copy(p_recv.at[source], p_recv.at[source], p_rsem.at[source]).wait()

    levels = []
    for j in range(half):
        packed = p_recv[j, :, hpd * hd:hpd * hd + LANES].astype(jnp.float32)
        levels.append(packed + pltpu.roll(packed, 96, 1) + pltpu.roll(packed, 64, 1))
    peak = functools.reduce(jnp.maximum, levels)
    factors = [jnp.exp2(level - peak) for level in levels]
    inverse = 1.0 / functools.reduce(jnp.add, factors)
    for i in range(hpd):
        total = jnp.zeros((n, hd), jnp.float32)
        for j in range(half):
            total += factors[j][:, i:i + 1] * p_recv[j, :, i * hd:(i + 1) * hd].astype(jnp.float32)
        att[:, i * hd:(i + 1) * hd] = (total * inverse[:, i:i + 1]).astype(jnp.bfloat16)

    def core_copy(k):
        return pltpu.make_async_remote_copy(
            src_ref=c_send.at[k], dst_ref=c_recv.at[k], send_sem=c_ssem.at[k], recv_sem=c_rsem.at[k],
            device_id=(seg, mate), device_id_type=MESH)

    def final_copy(j, k):
        return pltpu.make_async_remote_copy(
            src_ref=f_send.at[k, j], dst_ref=f_recv.at[k, pair],
            send_sem=f_ssem.at[k, j], recv_sem=f_rsem.at[k, pair],
            device_id=(ahead, 2 * j + core), device_id_type=MESH)

    @pl.loop(0, CHUNKS + 1)
    def _(step):
        @pl.when(step < CHUNKS)
        def _():
            weight_copy(step).wait()
            product = jnp.dot(att[...], w_buf[step], preferred_element_type=jnp.float32)
            own_sum[step, 0] = product[0:half]
            own_sum[step, 1] = product[half:n]
            other = own_sum[step, 1 - core]
            c_send[step] = jnp.concatenate(
                [other[:, 0:cols // 2], other[:, cols // 2:]], axis=0).astype(jnp.bfloat16)
            core_copy(step).start()

        @pl.when(step > 0)
        def _():
            k = step - 1
            core_copy(k).wait_recv()
            theirs = c_recv[k].astype(jnp.float32)
            both = own_sum[k, core] + jnp.concatenate([theirs[0:half], theirs[half:n]], axis=1)
            for b in range(blocks):
                t_scr[b * half:(b + 1) * half, :] = both[:, b * LANES:(b + 1) * LANES]
            for j in range(half):
                f_send[k, j] = t_scr[pl.ds(j, blocks, stride=half), :].astype(jnp.bfloat16)

            @pl.loop(0, half)
            def _(j):
                final_copy(lax.rem(pair + j, half), k).start()

    @pl.loop(0, CHUNKS)
    def _(k):
        @pl.loop(0, half)
        def _(j):
            pltpu.make_async_copy(f_recv.at[k, j], f_recv.at[k, j], f_rsem.at[k, j]).wait()

        total = f_recv[k, 0].astype(jnp.float32)
        for j in range(1, half):
            total += f_recv[k, j].astype(jnp.float32)
        out_ref[k] = total.astype(jnp.bfloat16)

    @pl.loop(1, n)
    def _(k):
        query_copy(k).wait_send()
        mask_copy(k).wait_send()

    @pl.loop(1, half)
    def _(k):
        part_copy(lax.rem(pair + k, half)).wait_send()

    @pl.loop(0, CHUNKS)
    def _(k):
        core_copy(k).wait_send()

        @pl.loop(0, half)
        def _(j):
            final_copy(j, k).wait_send()


def local(queries, page_ids, key_pages, value_pages, out_weight):
    n = lax.axis_size("dev")
    segments = lax.axis_size("segment")
    kv_heads, chosen = page_ids.shape[1:]
    pool, page, hd = key_pages.shape
    group = queries.shape[1] // (kv_heads * hd)
    depth, width = out_weight.shape
    half = n // 2
    hpd = kv_heads * group // n
    per_kv = group // 2
    tokens = pool * page
    cols = width // CHUNKS
    blocks = cols // LANES
    dims = (n, segments, kv_heads, chosen, pool, page, hd, group, width)
    bf16, f32 = jnp.bfloat16, jnp.float32
    dma = pltpu.SemaphoreType.DMA
    vmem = pltpu.VMEM
    out = pl.pallas_call(
        functools.partial(kernel, dims),
        out_shape=jax.ShapeDtypeStruct((CHUNKS, blocks, LANES), bf16),
        in_specs=[pl.BlockSpec(memory_space=pltpu.VMEM)] * 2 + [pl.BlockSpec(memory_space=pl.ANY)] * 3,
        out_specs=pl.BlockSpec(memory_space=pltpu.VMEM),
        scratch_shapes=[
            vmem((CHUNKS, depth, cols), bf16),
            vmem((2 * tokens, hd), bf16),
            vmem((2 * tokens, hd), bf16),
            vmem((2 * tokens, LANES), bf16),
            vmem((2, kv_heads * per_kv, hd), bf16),
            vmem((2, kv_heads * per_kv, hd), f32),
            vmem((half, 1, LANES), f32),
            vmem((n, kv_heads * per_kv, hd), bf16),
            vmem((n, 1, LANES), f32),
            vmem((kv_heads, n * per_kv, hd + LANES), bf16),
            vmem((2, 16 * per_kv, LANES), f32),
            vmem((half, n, hpd * hd + LANES), bf16),
            vmem((half, n, hpd * hd + LANES), bf16),
            vmem((n, hpd * hd), bf16),
            vmem((CHUNKS, 2, half, cols), f32),
            vmem((CHUNKS, n, cols // 2), bf16),
            vmem((CHUNKS, n, cols // 2), bf16),
            vmem((blocks * half, LANES), f32),
            vmem((CHUNKS, half, blocks, LANES), bf16),
            vmem((CHUNKS, half, blocks, LANES), bf16),
            dma((CHUNKS,)), dma((2,)), dma((2,)), dma((2,)),
            dma((n,)), dma((n,)), dma((n,)), dma((n,)),
            dma((half,)), dma((half,)),
            dma((CHUNKS,)), dma((CHUNKS,)),
            dma((CHUNKS, half)), dma((CHUNKS, half)),
        ],
        compiler_params=pltpu.CompilerParams(
            collective_id=0, has_side_effects=True, vmem_limit_bytes=56 * 1024 * 1024),
    )(queries, page_ids, key_pages.reshape(tokens, hd), value_pages.reshape(tokens, hd), out_weight)
    return out.reshape(1, width)


def solution(mesh):
    placed = (
        P(("segment", "dev"), None),
        P(("segment", "dev"), None, None),
        P(("segment", "dev"), None, None),
        P(("segment", "dev"), None, None),
        P(("segment", "dev"), None),
    )
    return jax.shard_map(
        local, mesh=mesh, in_specs=placed, out_specs=P(("segment", "dev"), None), check_vma=False
    )
```

```python
import functools
import math

import jax
import jax.numpy as jnp
from jax import lax
from jax.experimental import pallas as pl
from jax.experimental.pallas import tpu as pltpu
from jax.sharding import PartitionSpec as P

MESH = pl.DeviceIdType.MESH
LANES = 128
CHUNKS = 4
BIG = float(2.0**100)


def kernel(dims, q_ref, ids_ref, key_ref, value_ref, weight_ref, out_ref,
           q_in, ids_in, w_buf, k_buf, v_buf, key_t, q_stage, q32, m_stage, q_buf, m_buf, q_aug, o_scr,
           p_send, p_recv, att, own_sum, c_send, c_recv, y_sum, y_send, y_recv, t_scr, f_send, f_recv,
           in_sem, w_sem, kv_sem, kv_send, kv_recv, q_ssem, q_rsem, m_ssem, m_rsem, p_ssem, p_rsem,
           c_ssem, c_rsem, y_ssem, y_rsem, f_ssem, f_rsem):
    n, segments, kv_heads, chosen, pool, page, hd, group, width = dims
    half = n // 2
    quarter = half // 2
    hpd = kv_heads * group // n
    per_kv = group // 2
    tokens = pool * page
    span = 2 * pool
    cols = width // CHUNKS
    blocks = cols // LANES
    seg = lax.axis_index("segment")
    me = lax.axis_index("dev")
    core = lax.rem(me, 2)
    pair = me // 2
    mate = me + 1 - 2 * core
    side = lax.rem(pair, 2)
    level_of = pair // 2
    across = 2 * (pair + 1 - 2 * side) + core
    slot = core * half + side * quarter + level_of
    ahead = lax.rem(seg + 1, segments)
    behind = lax.rem(seg + segments - 1, segments)

    def weight_copy(k):
        return pltpu.make_async_copy(
            weight_ref.at[:, pl.ds(pl.multiple_of(k * cols, cols), cols)], w_buf.at[k], w_sem.at[k])

    query_in = pltpu.make_async_copy(q_ref, q_in, in_sem.at[0])
    page_in = pltpu.make_async_copy(ids_ref, ids_in, in_sem.at[1])
    query_in.start()
    page_in.start()

    barrier = pltpu.get_barrier_semaphore()

    @pl.loop(1, n)
    def _(k):
        pl.semaphore_signal(barrier, inc=1, device_id=(seg, lax.rem(me + k, n)), device_id_type=MESH)

    @pl.loop(0, quarter)
    def _(j):
        pl.semaphore_signal(barrier, inc=1, device_id=(behind, 4 * j + 2 * side + core), device_id_type=MESH)

    here = pl.ds(pl.multiple_of(core * tokens, tokens), tokens)
    key_local = pltpu.make_async_copy(key_ref, k_buf.at[here], kv_sem.at[0])
    value_local = pltpu.make_async_copy(value_ref, v_buf.at[here], kv_sem.at[1])
    key_local.start()
    value_local.start()

    @pl.loop(0, CHUNKS)
    def _(k):
        weight_copy(k).start()

    query_in.wait()
    page_in.wait()

    for c in range(2):
        for h in range(kv_heads):
            for u in range(per_kv // hpd):
                for i in range(hpd):
                    head = h * group + u * 2 * hpd + c * hpd + i
                    place = h * per_kv + u * hpd + i
                    q32[c, place:place + 1, :] = q_in[0:1, head * hd:(head + 1) * hd].astype(jnp.float32)
    q_stage[...] = q32[...].astype(jnp.bfloat16)

    head_of_lane = lax.broadcasted_iota(jnp.int32, (kv_heads, LANES), 1) // span
    pick = (head_of_lane == lax.broadcasted_iota(jnp.int32, (kv_heads, LANES), 0)).astype(jnp.float32)
    ids = ids_in[0].astype(jnp.float32)
    spread = lax.dot_general(ids, pick, (((0,), (0,)), ((), ())),
                             precision=lax.Precision.HIGHEST, preferred_element_type=jnp.float32)
    in_span = lax.rem(lax.broadcasted_iota(jnp.int32, (chosen, LANES), 1), span).astype(jnp.float32)
    offset = spread - in_span
    for j in range(half):
        hit = (jnp.abs(offset - float(j * span)) < 0.5).astype(jnp.float32)
        m_stage[j] = jnp.max(hit, axis=0, keepdims=True)

    q_buf[slot] = q_stage[core]
    m_buf[slot] = m_stage[pair]

    key_local.wait()
    value_local.wait()
    lane_page = lax.rem(lax.broadcasted_iota(jnp.int32, (LANES, 2 * tokens), 0), span)
    token_page = lax.broadcasted_iota(jnp.int32, (LANES, 2 * tokens), 1) // page
    key_t[hd:hd + LANES, :] = jnp.where(lane_page == token_page, BIG, 0.0).astype(jnp.bfloat16)
    key_t[0:hd, here] = k_buf[here, :].T

    pl.semaphore_wait(barrier, n - 1 + quarter)

    def query_copy(k):
        peer = lax.rem(me + k, n)
        return pltpu.make_async_remote_copy(
            src_ref=q_stage.at[lax.rem(peer, 2)], dst_ref=q_buf.at[slot],
            send_sem=q_ssem.at[k], recv_sem=q_rsem.at[slot],
            device_id=(seg, peer), device_id_type=MESH)

    def mask_copy(k):
        peer = lax.rem(me + k, n)
        return pltpu.make_async_remote_copy(
            src_ref=m_stage.at[peer // 2], dst_ref=m_buf.at[slot],
            send_sem=m_ssem.at[k], recv_sem=m_rsem.at[slot],
            device_id=(seg, peer), device_id_type=MESH)

    key_remote = pltpu.make_async_remote_copy(
        src_ref=k_buf.at[here], dst_ref=k_buf.at[here], send_sem=kv_send.at[0], recv_sem=kv_recv.at[0],
        device_id=(seg, mate), device_id_type=MESH)
    value_remote = pltpu.make_async_remote_copy(
        src_ref=v_buf.at[here], dst_ref=v_buf.at[here], send_sem=kv_send.at[1], recv_sem=kv_recv.at[1],
        device_id=(seg, mate), device_id_type=MESH)
    key_remote.start()
    value_remote.start()

    @pl.loop(1, n)
    def _(k):
        query_copy(k).start()
        mask_copy(k).start()

    key_remote.wait()
    there = pl.ds(pl.multiple_of((1 - core) * tokens, tokens), tokens)
    key_t[0:hd, there] = k_buf[there, :].T
    value_remote.wait()

    @pl.loop(1, n)
    def _(k):
        source = lax.rem(me + n - k, n)
        place = lax.rem(source, 2) * half + lax.rem(source // 2, 2) * quarter + source // 4
        pltpu.make_async_copy(q_buf.at[place], q_buf.at[place], q_rsem.at[place]).wait()
        pltpu.make_async_copy(m_buf.at[place], m_buf.at[place], m_rsem.at[place]).wait()

    lane3 = lax.broadcasted_iota(jnp.int32, (n, 1, LANES), 2) // span
    absent = m_buf[...] - 1.0
    all_q = q_buf[...].astype(jnp.float32)
    for h in range(kv_heads):
        bias = jnp.where(lane3 == h, absent, 0.0)
        bias = jnp.broadcast_to(bias, (n, per_kv, LANES)).reshape(n * per_kv, LANES)
        q_aug[h, :, 0:hd] = all_q[:, h * per_kv:(h + 1) * per_kv, :].reshape(n * per_kv, hd).astype(jnp.bfloat16)
        q_aug[h, :, hd:hd + LANES] = bias.astype(jnp.bfloat16)

    def part_copy(j):
        return pltpu.make_async_remote_copy(
            src_ref=p_send.at[j], dst_ref=p_recv.at[pair],
            send_sem=p_ssem.at[j], recv_sem=p_rsem.at[pair],
            device_id=(seg, 2 * j + core), device_id_type=MESH)

    scale = math.log2(math.e) / math.sqrt(hd)
    lane = lax.broadcasted_iota(jnp.int32, (16, LANES), 1)
    units = per_kv // hpd

    tiles = [(h, rb) for h in range(kv_heads) for rb in range(n // 16)]

    def score(h, rb):
        queries = q_aug[h, rb * 16 * per_kv:(rb + 1) * 16 * per_kv, :]
        return jnp.dot(queries, key_t[...], preferred_element_type=jnp.float32)

    values = jnp.concatenate([v_buf[...], jnp.ones((2 * tokens, LANES), jnp.bfloat16)], axis=1)
    scores = score(*tiles[0])
    for index_of, (h, rb) in enumerate(tiles):
            upcoming = score(*tiles[index_of + 1]) if index_of + 1 < len(tiles) else None
            top = jnp.max(scores, axis=1, keepdims=True) * scale
            weights = jnp.exp2(scores * scale - top).astype(jnp.bfloat16)
            sums = jnp.dot(weights, values, preferred_element_type=jnp.float32)
            o_scr[0] = sums[:, 0:hd] / sums[:, hd:]
            o_scr[1] = top + jnp.log2(sums[:, hd:])
            rows = slice(rb * 16, (rb + 1) * 16)
            for u in range(units):
                level = jnp.zeros((16, LANES), jnp.float32)
                for i in range(hpd):
                    index = u * hpd + i
                    value = o_scr[0, pl.ds(index, 16, stride=per_kv), :]
                    p_send[h * units + u, rows, i * hd:(i + 1) * hd] = value.astype(jnp.bfloat16)
                    level = jnp.where(lax.rem(lane, 32) == i, o_scr[1, pl.ds(index, 16, stride=per_kv), :], level)
                high = level.astype(jnp.bfloat16)
                rest = level - high.astype(jnp.float32)
                middle = rest.astype(jnp.bfloat16)
                low = rest - middle.astype(jnp.float32)
                packed = jnp.where(lane < 32, high.astype(jnp.float32),
                                   jnp.where(lane < 64, middle.astype(jnp.float32), low))
                p_send[h * units + u, rows, hpd * hd:hpd * hd + LANES] = packed.astype(jnp.bfloat16)
            scores = upcoming
            if rb + 1 < n // 16:
                continue
            for u in range(units):
                j = h * units + u

                @pl.when(j != pair)
                def _(j=j):
                    part_copy(j).start()

                @pl.when(j == pair)
                def _(j=j):
                    p_recv[pair] = p_send[j]

    @pl.loop(1, n)
    def _(k):
        query_copy(k).wait_send()
        mask_copy(k).wait_send()

    @pl.loop(1, half)
    def _(k):
        source = lax.rem(pair + half - k, half)
        pltpu.make_async_copy(p_recv.at[source], p_recv.at[source], p_rsem.at[source]).wait()

    levels = []
    for j in range(half):
        packed = p_recv[j, :, hpd * hd:hpd * hd + LANES].astype(jnp.float32)
        levels.append(packed + pltpu.roll(packed, 96, 1) + pltpu.roll(packed, 64, 1))
    peak = functools.reduce(jnp.maximum, levels)
    factors = [jnp.exp2(level - peak) for level in levels]
    inverse = 1.0 / functools.reduce(jnp.add, factors)
    for i in range(hpd):
        total = jnp.zeros((n, hd), jnp.float32)
        for j in range(half):
            total += factors[j][:, i:i + 1] * p_recv[j, :, i * hd:(i + 1) * hd].astype(jnp.float32)
        att[:, i * hd:(i + 1) * hd] = (total * inverse[:, i:i + 1]).astype(jnp.bfloat16)

    def core_copy(k):
        return pltpu.make_async_remote_copy(
            src_ref=c_send.at[k], dst_ref=c_recv.at[k], send_sem=c_ssem.at[k], recv_sem=c_rsem.at[k],
            device_id=(seg, mate), device_id_type=MESH)

    def side_copy(k):
        return pltpu.make_async_remote_copy(
            src_ref=y_send.at[k], dst_ref=y_recv.at[k], send_sem=y_ssem.at[k], recv_sem=y_rsem.at[k],
            device_id=(seg, across), device_id_type=MESH)

    def final_copy(j, k):
        return pltpu.make_async_remote_copy(
            src_ref=f_send.at[k, j], dst_ref=f_recv.at[k, level_of],
            send_sem=f_ssem.at[k, j], recv_sem=f_rsem.at[k, level_of],
            device_id=(ahead, 4 * j + 2 * side + core), device_id_type=MESH)

    pieces = max(1, 16 // quarter)
    piece = cols // pieces

    @pl.loop(0, CHUNKS + 2)
    def _(step):
        @pl.when(step < CHUNKS)
        def _():
            weight_copy(step).wait()
            product = jnp.dot(att[...], w_buf[step], preferred_element_type=jnp.float32)
            own_sum[step, 0] = product[0:half]
            own_sum[step, 1] = product[half:n]
            other = own_sum[step, 1 - core]
            c_send[step] = jnp.concatenate(
                [other[:, 0:cols // 2], other[:, cols // 2:]], axis=0).astype(jnp.bfloat16)
            core_copy(step).start()

        @pl.when((step > 0) & (step <= CHUNKS))
        def _():
            k = step - 1
            core_copy(k).wait_recv()
            theirs = c_recv[k].astype(jnp.float32)
            both = own_sum[k, core] + jnp.concatenate([theirs[0:half], theirs[half:n]], axis=1)
            y_sum[k, 0] = both[0:quarter]
            y_sum[k, 1] = both[quarter:half]
            other = y_sum[k, 1 - side]
            y_send[k] = jnp.concatenate(
                [other[:, p * piece:(p + 1) * piece] for p in range(pieces)], axis=0).astype(jnp.bfloat16)
            side_copy(k).start()

        @pl.when(step > 1)
        def _():
            k = step - 2
            side_copy(k).wait_recv()
            theirs = y_recv[k].astype(jnp.float32)
            both = y_sum[k, side] + jnp.concatenate(
                [theirs[p * quarter:(p + 1) * quarter] for p in range(pieces)], axis=1)
            for b in range(blocks):
                t_scr[b * quarter:(b + 1) * quarter, :] = both[:, b * LANES:(b + 1) * LANES]
            for j in range(quarter):
                f_send[k, j] = t_scr[pl.ds(j, blocks, stride=quarter), :].astype(jnp.bfloat16)

            @pl.loop(0, quarter)
            def _(j):
                final_copy(lax.rem(level_of + 1 + j, quarter), k).start()

    @pl.loop(1, half)
    def _(k):
        part_copy(lax.rem(pair + k, half)).wait_send()

    @pl.loop(0, CHUNKS)
    def _(k):
        core_copy(k).wait_send()
        side_copy(k).wait_send()

    for k in range(CHUNKS):
        @pl.loop(0, quarter)
        def _(j, k=k):
            pltpu.make_async_copy(f_recv.at[k, j], f_recv.at[k, j], f_rsem.at[k, j]).wait()

        total = f_recv[k, 0].astype(jnp.float32)
        for j in range(1, quarter):
            total += f_recv[k, j].astype(jnp.float32)
        out_ref[k] = total.astype(jnp.bfloat16)

        @pl.loop(0, quarter)
        def _(j, k=k):
            final_copy(j, k).wait_send()


def local(queries, page_ids, key_pages, value_pages, out_weight):
    n = lax.axis_size("dev")
    segments = lax.axis_size("segment")
    kv_heads, chosen = page_ids.shape[1:]
    pool, page, hd = key_pages.shape
    group = queries.shape[1] // (kv_heads * hd)
    depth, width = out_weight.shape
    half = n // 2
    quarter = half // 2
    pieces = max(1, 16 // quarter)
    hpd = kv_heads * group // n
    per_kv = group // 2
    tokens = pool * page
    cols = width // CHUNKS
    blocks = cols // LANES
    dims = (n, segments, kv_heads, chosen, pool, page, hd, group, width)
    bf16, f32 = jnp.bfloat16, jnp.float32
    dma = pltpu.SemaphoreType.DMA
    vmem = pltpu.VMEM
    out = pl.pallas_call(
        functools.partial(kernel, dims),
        out_shape=jax.ShapeDtypeStruct((CHUNKS, blocks, LANES), bf16),
        in_specs=[pl.BlockSpec(memory_space=pl.ANY)] * 5,
        out_specs=pl.BlockSpec(memory_space=pltpu.VMEM),
        scratch_shapes=[
            vmem(queries.shape, bf16),
            vmem(page_ids.shape, jnp.int32),
            vmem((CHUNKS, depth, cols), bf16),
            vmem((2 * tokens, hd), bf16),
            vmem((2 * tokens, hd), bf16),
            vmem((hd + LANES, 2 * tokens), bf16),
            vmem((2, kv_heads * per_kv, hd), bf16),
            vmem((2, kv_heads * per_kv, hd), f32),
            vmem((half, 1, LANES), f32),
            vmem((n, kv_heads * per_kv, hd), bf16),
            vmem((n, 1, LANES), f32),
            vmem((kv_heads, n * per_kv, hd + LANES), bf16),
            vmem((2, 16 * per_kv, LANES), f32),
            vmem((half, n, hpd * hd + LANES), bf16),
            vmem((half, n, hpd * hd + LANES), bf16),
            vmem((n, hpd * hd), bf16),
            vmem((CHUNKS, 2, half, cols), f32),
            vmem((CHUNKS, n, cols // 2), bf16),
            vmem((CHUNKS, n, cols // 2), bf16),
            vmem((CHUNKS, 2, quarter, cols), f32),
            vmem((CHUNKS, pieces * quarter, cols // pieces), bf16),
            vmem((CHUNKS, pieces * quarter, cols // pieces), bf16),
            vmem((blocks * quarter, LANES), f32),
            vmem((CHUNKS, quarter, blocks, LANES), bf16),
            vmem((CHUNKS, quarter, blocks, LANES), bf16),
            dma((2,)), dma((CHUNKS,)), dma((2,)), dma((2,)), dma((2,)),
            dma((n,)), dma((n,)), dma((n,)), dma((n,)),
            dma((half,)), dma((half,)),
            dma((CHUNKS,)), dma((CHUNKS,)), dma((CHUNKS,)), dma((CHUNKS,)),
            dma((CHUNKS, quarter)), dma((CHUNKS, quarter)),
        ],
        compiler_params=pltpu.CompilerParams(
            collective_id=0, has_side_effects=True, vmem_limit_bytes=56 * 1024 * 1024),
    )(queries, page_ids, key_pages.reshape(tokens, hd), value_pages.reshape(tokens, hd), out_weight)
    return out.reshape(1, width)


def solution(mesh):
    placed = (
        P(("segment", "dev"), None),
        P(("segment", "dev"), None, None),
        P(("segment", "dev"), None, None),
        P(("segment", "dev"), None, None),
        P(("segment", "dev"), None),
    )
    return jax.shard_map(
        local, mesh=mesh, in_specs=placed, out_specs=P(("segment", "dev"), None), check_vma=False
    )
```

```python
import functools
import math

import jax
import jax.numpy as jnp
from jax import lax
from jax.experimental import pallas as pl
from jax.experimental.pallas import tpu as pltpu
from jax.sharding import PartitionSpec as P

MESH = pl.DeviceIdType.MESH
LANES = 128
CHUNKS = 4
BIG = float(2.0**100)


def kernel(dims, q_ref, ids_ref, key_ref, value_ref, weight_ref, out_ref,
           q_in, ids_in, w_buf, k_buf, v_buf, key_t, q_stage, q32, m_stage, q_buf, m_buf, q_aug, o_scr,
           p_send, p_recv, att, own_sum, c_send, c_recv, y_sum, y_send, y_recv, t_scr, f_send, f_recv,
           in_sem, w_sem, kv_sem, kv_send, kv_recv, q_ssem, q_rsem, m_ssem, m_rsem, p_ssem, p_rsem,
           c_ssem, c_rsem, y_ssem, y_rsem, f_ssem, f_rsem):
    n, segments, kv_heads, chosen, pool, page, hd, group, width = dims
    half = n // 2
    quarter = half // 2
    hpd = kv_heads * group // n
    per_kv = group // 2
    tokens = pool * page
    span = 2 * pool
    cols = width // CHUNKS
    blocks = cols // LANES
    seg = lax.axis_index("segment")
    me = lax.axis_index("dev")
    core = lax.rem(me, 2)
    pair = me // 2
    mate = me + 1 - 2 * core
    side = lax.rem(pair, 2)
    level_of = pair // 2
    across = 2 * (pair + 1 - 2 * side) + core
    slot = core * half + side * quarter + level_of
    ahead = lax.rem(seg + 1, segments)
    behind = lax.rem(seg + segments - 1, segments)

    def weight_copy(k):
        return pltpu.make_async_copy(
            weight_ref.at[:, pl.ds(pl.multiple_of(k * cols, cols), cols)], w_buf.at[k], w_sem.at[k])

    query_in = pltpu.make_async_copy(q_ref, q_in, in_sem.at[0])
    page_in = pltpu.make_async_copy(ids_ref, ids_in, in_sem.at[1])
    query_in.start()
    page_in.start()

    barrier = pltpu.get_barrier_semaphore()

    @pl.loop(1, n)
    def _(k):
        pl.semaphore_signal(barrier, inc=1, device_id=(seg, lax.rem(me + k, n)), device_id_type=MESH)

    @pl.loop(0, quarter)
    def _(j):
        pl.semaphore_signal(barrier, inc=1, device_id=(behind, 4 * j + 2 * side + core), device_id_type=MESH)

    here = pl.ds(pl.multiple_of(core * tokens, tokens), tokens)
    key_local = pltpu.make_async_copy(key_ref, k_buf.at[here], kv_sem.at[0])
    value_local = pltpu.make_async_copy(value_ref, v_buf.at[here], kv_sem.at[1])
    key_local.start()
    value_local.start()

    query_in.wait()

    for c in range(2):
        for h in range(kv_heads):
            for u in range(per_kv // hpd):
                for i in range(hpd):
                    head = h * group + u * 2 * hpd + c * hpd + i
                    place = h * per_kv + u * hpd + i
                    q32[c, place:place + 1, :] = q_in[0:1, head * hd:(head + 1) * hd].astype(jnp.float32)
    q_stage[...] = q32[...].astype(jnp.bfloat16)

    q_buf[slot] = q_stage[core]

    pl.semaphore_wait(barrier, n - 1 + quarter)

    key_remote = pltpu.make_async_remote_copy(
        src_ref=key_ref, dst_ref=k_buf.at[here], send_sem=kv_send.at[0], recv_sem=kv_recv.at[0],
        device_id=(seg, mate), device_id_type=MESH)
    value_remote = pltpu.make_async_remote_copy(
        src_ref=value_ref, dst_ref=v_buf.at[here], send_sem=kv_send.at[1], recv_sem=kv_recv.at[1],
        device_id=(seg, mate), device_id_type=MESH)
    key_remote.start()
    value_remote.start()

    def query_copy(k):
        peer = lax.rem(me + k, n)
        return pltpu.make_async_remote_copy(
            src_ref=q_stage.at[lax.rem(peer, 2)], dst_ref=q_buf.at[slot],
            send_sem=q_ssem.at[k], recv_sem=q_rsem.at[slot],
            device_id=(seg, peer), device_id_type=MESH)

    def mask_copy(k):
        peer = lax.rem(me + k, n)
        return pltpu.make_async_remote_copy(
            src_ref=m_stage.at[peer // 2], dst_ref=m_buf.at[slot],
            send_sem=m_ssem.at[k], recv_sem=m_rsem.at[slot],
            device_id=(seg, peer), device_id_type=MESH)

    @pl.loop(1, n)
    def _(k):
        query_copy(k).start()

    @pl.loop(0, CHUNKS)
    def _(k):
        weight_copy(k).start()

    page_in.wait()

    head_of_lane = lax.broadcasted_iota(jnp.int32, (kv_heads, LANES), 1) // span
    pick = (head_of_lane == lax.broadcasted_iota(jnp.int32, (kv_heads, LANES), 0)).astype(jnp.float32)
    ids = ids_in[0].astype(jnp.float32)
    spread = lax.dot_general(ids, pick, (((0,), (0,)), ((), ())),
                             precision=lax.Precision.HIGHEST, preferred_element_type=jnp.float32)
    in_span = lax.rem(lax.broadcasted_iota(jnp.int32, (chosen, LANES), 1), span).astype(jnp.float32)
    offset = spread - in_span
    for j in range(half):
        hit = (jnp.abs(offset - float(j * span)) < 0.5).astype(jnp.float32)
        m_stage[j] = jnp.max(hit, axis=0, keepdims=True)

    m_buf[slot] = m_stage[pair]

    @pl.loop(1, n)
    def _(k):
        mask_copy(k).start()

    key_local.wait()
    value_local.wait()
    lane_page = lax.rem(lax.broadcasted_iota(jnp.int32, (LANES, LANES), 0), span)[:, 0:1]
    token_page = lax.broadcasted_iota(jnp.int32, (8, 2 * tokens), 1)[0:1] // page
    key_t[hd:hd + LANES, :] = jnp.where(lane_page == token_page, BIG, 0.0).astype(jnp.bfloat16)
    key_t[0:hd, here] = k_buf[here, :].T

    key_remote.wait()
    there = pl.ds(pl.multiple_of((1 - core) * tokens, tokens), tokens)
    key_t[0:hd, there] = k_buf[there, :].T
    value_remote.wait()

    @pl.loop(1, n)
    def _(k):
        source = lax.rem(me + n - k, n)
        place = lax.rem(source, 2) * half + lax.rem(source // 2, 2) * quarter + source // 4
        pltpu.make_async_copy(q_buf.at[place], q_buf.at[place], q_rsem.at[place]).wait()
        pltpu.make_async_copy(m_buf.at[place], m_buf.at[place], m_rsem.at[place]).wait()

    lane3 = lax.broadcasted_iota(jnp.int32, (n, 1, LANES), 2) // span
    absent = m_buf[...] - 1.0
    all_q = q_buf[...].astype(jnp.float32)
    for h in range(kv_heads):
        bias = jnp.where(lane3 == h, absent, 0.0)
        bias = jnp.broadcast_to(bias, (n, per_kv, LANES)).reshape(n * per_kv, LANES)
        q_aug[h, :, 0:hd] = all_q[:, h * per_kv:(h + 1) * per_kv, :].reshape(n * per_kv, hd).astype(jnp.bfloat16)
        q_aug[h, :, hd:hd + LANES] = bias.astype(jnp.bfloat16)

    def part_copy(j):
        return pltpu.make_async_remote_copy(
            src_ref=p_send.at[j], dst_ref=p_recv.at[pair],
            send_sem=p_ssem.at[j], recv_sem=p_rsem.at[pair],
            device_id=(seg, 2 * j + core), device_id_type=MESH)

    scale = math.log2(math.e) / math.sqrt(hd)
    lane = lax.broadcasted_iota(jnp.int32, (16, LANES), 1)
    units = per_kv // hpd

    @pl.loop(0, kv_heads)
    def _(h):
        values = jnp.concatenate([v_buf[...], jnp.ones((2 * tokens, LANES), jnp.bfloat16)], axis=1)
        for rb in range(n // 16):
            queries = q_aug[h, rb * 16 * per_kv:(rb + 1) * 16 * per_kv, :]
            scores = jnp.dot(queries, key_t[...], preferred_element_type=jnp.float32)
            top = jnp.max(scores, axis=1, keepdims=True) * scale
            weights = jnp.exp2(scores * scale - top).astype(jnp.bfloat16)
            sums = jnp.dot(weights, values, preferred_element_type=jnp.float32)
            o_scr[0] = sums[:, 0:hd] / sums[:, hd:]
            o_scr[1] = top + jnp.log2(sums[:, hd:])
            rows = slice(rb * 16, (rb + 1) * 16)
            for u in range(units):
                level = jnp.zeros((16, LANES), jnp.float32)
                for i in range(hpd):
                    index = u * hpd + i
                    value = o_scr[0, pl.ds(index, 16, stride=per_kv), :]
                    p_send[h * units + u, rows, i * hd:(i + 1) * hd] = value.astype(jnp.bfloat16)
                    level = jnp.where(lax.rem(lane, 32) == i, o_scr[1, pl.ds(index, 16, stride=per_kv), :], level)
                high = level.astype(jnp.bfloat16)
                rest = level - high.astype(jnp.float32)
                middle = rest.astype(jnp.bfloat16)
                low = rest - middle.astype(jnp.float32)
                packed = jnp.where(lane < 32, high.astype(jnp.float32),
                                   jnp.where(lane < 64, middle.astype(jnp.float32), low))
                p_send[h * units + u, rows, hpd * hd:hpd * hd + LANES] = packed.astype(jnp.bfloat16)
        for u in range(units):
            j = h * units + u

            @pl.when(j != pair)
            def _():
                part_copy(j).start()

            @pl.when(j == pair)
            def _():
                p_recv[pair] = p_send[j]

    @pl.loop(1, n)
    def _(k):
        query_copy(k).wait_send()
        mask_copy(k).wait_send()

    @pl.loop(1, half)
    def _(k):
        source = lax.rem(pair + half - k, half)
        pltpu.make_async_copy(p_recv.at[source], p_recv.at[source], p_rsem.at[source]).wait()

    levels = []
    for j in range(half):
        packed = p_recv[j, :, hpd * hd:hpd * hd + LANES].astype(jnp.float32)
        levels.append(packed + pltpu.roll(packed, 96, 1) + pltpu.roll(packed, 64, 1))
    peak = functools.reduce(jnp.maximum, levels)
    factors = [jnp.exp2(level - peak) for level in levels]
    inverse = 1.0 / functools.reduce(jnp.add, factors)
    for i in range(hpd):
        total = jnp.zeros((n, hd), jnp.float32)
        for j in range(half):
            total += factors[j][:, i:i + 1] * p_recv[j, :, i * hd:(i + 1) * hd].astype(jnp.float32)
        att[:, i * hd:(i + 1) * hd] = (total * inverse[:, i:i + 1]).astype(jnp.bfloat16)

    def core_copy(k):
        return pltpu.make_async_remote_copy(
            src_ref=c_send.at[k], dst_ref=c_recv.at[k], send_sem=c_ssem.at[k], recv_sem=c_rsem.at[k],
            device_id=(seg, mate), device_id_type=MESH)

    def side_copy(k):
        return pltpu.make_async_remote_copy(
            src_ref=y_send.at[k], dst_ref=y_recv.at[k], send_sem=y_ssem.at[k], recv_sem=y_rsem.at[k],
            device_id=(seg, across), device_id_type=MESH)

    def final_copy(j, k):
        return pltpu.make_async_remote_copy(
            src_ref=f_send.at[k, j], dst_ref=f_recv.at[k, level_of],
            send_sem=f_ssem.at[k, j], recv_sem=f_rsem.at[k, level_of],
            device_id=(ahead, 4 * j + 2 * side + core), device_id_type=MESH)

    pieces = max(1, 16 // quarter)
    piece = cols // pieces

    @pl.loop(0, CHUNKS + 2)
    def _(step):
        @pl.when(step < CHUNKS)
        def _():
            weight_copy(step).wait()
            product = jnp.dot(att[...], w_buf[step], preferred_element_type=jnp.float32)
            own_sum[step, 0] = product[0:half]
            own_sum[step, 1] = product[half:n]
            other = own_sum[step, 1 - core]
            c_send[step] = jnp.concatenate(
                [other[:, 0:cols // 2], other[:, cols // 2:]], axis=0).astype(jnp.bfloat16)
            core_copy(step).start()

        @pl.when((step > 0) & (step <= CHUNKS))
        def _():
            k = step - 1
            core_copy(k).wait_recv()
            theirs = c_recv[k].astype(jnp.float32)
            both = own_sum[k, core] + jnp.concatenate([theirs[0:half], theirs[half:n]], axis=1)
            y_sum[k, 0] = both[0:quarter]
            y_sum[k, 1] = both[quarter:half]
            other = y_sum[k, 1 - side]
            y_send[k] = jnp.concatenate(
                [other[:, p * piece:(p + 1) * piece] for p in range(pieces)], axis=0).astype(jnp.bfloat16)
            side_copy(k).start()

        @pl.when(step > 1)
        def _():
            k = step - 2
            side_copy(k).wait_recv()
            theirs = y_recv[k].astype(jnp.float32)
            both = y_sum[k, side] + jnp.concatenate(
                [theirs[p * quarter:(p + 1) * quarter] for p in range(pieces)], axis=1)
            for b in range(blocks):
                t_scr[b * quarter:(b + 1) * quarter, :] = both[:, b * LANES:(b + 1) * LANES]
            for j in range(quarter):
                f_send[k, j] = t_scr[pl.ds(j, blocks, stride=quarter), :].astype(jnp.bfloat16)

            @pl.loop(0, quarter)
            def _(j):
                final_copy(lax.rem(level_of + 1 + j, quarter), k).start()

    @pl.loop(1, half)
    def _(k):
        part_copy(lax.rem(pair + k, half)).wait_send()

    @pl.loop(0, CHUNKS)
    def _(k):
        core_copy(k).wait_send()
        side_copy(k).wait_send()

    for k in range(CHUNKS):
        @pl.loop(0, quarter)
        def _(j, k=k):
            pltpu.make_async_copy(f_recv.at[k, j], f_recv.at[k, j], f_rsem.at[k, j]).wait()

        total = f_recv[k, 0].astype(jnp.float32)
        for j in range(1, quarter):
            total += f_recv[k, j].astype(jnp.float32)
        out_ref[k] = total.astype(jnp.bfloat16)

        @pl.loop(0, quarter)
        def _(j, k=k):
            final_copy(j, k).wait_send()


def local(queries, page_ids, key_pages, value_pages, out_weight):
    n = lax.axis_size("dev")
    segments = lax.axis_size("segment")
    kv_heads, chosen = page_ids.shape[1:]
    pool, page, hd = key_pages.shape
    group = queries.shape[1] // (kv_heads * hd)
    depth, width = out_weight.shape
    half = n // 2
    quarter = half // 2
    pieces = max(1, 16 // quarter)
    hpd = kv_heads * group // n
    per_kv = group // 2
    tokens = pool * page
    cols = width // CHUNKS
    blocks = cols // LANES
    dims = (n, segments, kv_heads, chosen, pool, page, hd, group, width)
    bf16, f32 = jnp.bfloat16, jnp.float32
    dma = pltpu.SemaphoreType.DMA
    vmem = pltpu.VMEM
    out = pl.pallas_call(
        functools.partial(kernel, dims),
        out_shape=jax.ShapeDtypeStruct((CHUNKS, blocks, LANES), bf16),
        in_specs=[pl.BlockSpec(memory_space=pl.ANY)] * 5,
        out_specs=pl.BlockSpec(memory_space=pltpu.VMEM),
        scratch_shapes=[
            vmem(queries.shape, bf16),
            vmem(page_ids.shape, jnp.int32),
            vmem((CHUNKS, depth, cols), bf16),
            vmem((2 * tokens, hd), bf16),
            vmem((2 * tokens, hd), bf16),
            vmem((hd + LANES, 2 * tokens), bf16),
            vmem((2, kv_heads * per_kv, hd), bf16),
            vmem((2, kv_heads * per_kv, hd), f32),
            vmem((half, 1, LANES), f32),
            vmem((n, kv_heads * per_kv, hd), bf16),
            vmem((n, 1, LANES), f32),
            vmem((kv_heads, n * per_kv, hd + LANES), bf16),
            vmem((2, 16 * per_kv, LANES), f32),
            vmem((half, n, hpd * hd + LANES), bf16),
            vmem((half, n, hpd * hd + LANES), bf16),
            vmem((n, hpd * hd), bf16),
            vmem((CHUNKS, 2, half, cols), f32),
            vmem((CHUNKS, n, cols // 2), bf16),
            vmem((CHUNKS, n, cols // 2), bf16),
            vmem((CHUNKS, 2, quarter, cols), f32),
            vmem((CHUNKS, pieces * quarter, cols // pieces), bf16),
            vmem((CHUNKS, pieces * quarter, cols // pieces), bf16),
            vmem((blocks * quarter, LANES), f32),
            vmem((CHUNKS, quarter, blocks, LANES), bf16),
            vmem((CHUNKS, quarter, blocks, LANES), bf16),
            dma((2,)), dma((CHUNKS,)), dma((2,)), dma((2,)), dma((2,)),
            dma((n,)), dma((n,)), dma((n,)), dma((n,)),
            dma((half,)), dma((half,)),
            dma((CHUNKS,)), dma((CHUNKS,)), dma((CHUNKS,)), dma((CHUNKS,)),
            dma((CHUNKS, quarter)), dma((CHUNKS, quarter)),
        ],
        compiler_params=pltpu.CompilerParams(
            collective_id=0, has_side_effects=True, vmem_limit_bytes=56 * 1024 * 1024),
    )(queries, page_ids, key_pages.reshape(tokens, hd), value_pages.reshape(tokens, hd), out_weight)
    return out.reshape(1, width)


def solution(mesh):
    placed = (
        P(("segment", "dev"), None),
        P(("segment", "dev"), None, None),
        P(("segment", "dev"), None, None),
        P(("segment", "dev"), None, None),
        P(("segment", "dev"), None),
    )
    return jax.shard_map(
        local, mesh=mesh, in_specs=placed, out_specs=P(("segment", "dev"), None), check_vma=False
    )
```

```python
import functools
import math

import jax
import jax.numpy as jnp
from jax import lax
from jax.experimental import pallas as pl
from jax.experimental.pallas import tpu as pltpu
from jax.sharding import PartitionSpec as P

MESH = pl.DeviceIdType.MESH
LANES = 128
CHUNKS = 4
BIG = float(2.0**100)


def kernel(dims, q_ref, ids_ref, key_ref, value_ref, weight_ref, out_ref,
           q_in, ids_in, w_buf, k_buf, v_buf, page_hot, q_stage, q32, m_stage, q_buf, m_buf, q_aug, o_scr,
           p_send, p_recv, att, own_sum, c_send, c_recv, t_scr, f_send, f_recv,
           in_sem, w_sem, kv_sem, kv_send, kv_recv, q_ssem, q_rsem, m_ssem, m_rsem, p_ssem, p_rsem,
           c_ssem, c_rsem, f_ssem, f_rsem):
    n, segments, kv_heads, chosen, pool, page, hd, group, width = dims
    half = n // 2
    hpd = kv_heads * group // n
    per_kv = group // 2
    tokens = pool * page
    span = 2 * pool
    cols = width // CHUNKS
    blocks = cols // LANES
    seg = lax.axis_index("segment")
    me = lax.axis_index("dev")
    core = lax.rem(me, 2)
    pair = me // 2
    mate = me + 1 - 2 * core
    slot = core * half + pair
    ahead = lax.rem(seg + 1, segments)
    behind = lax.rem(seg + segments - 1, segments)

    def weight_copy(k):
        return pltpu.make_async_copy(
            weight_ref.at[:, pl.ds(pl.multiple_of(k * cols, cols), cols)], w_buf.at[k], w_sem.at[k])

    query_in = pltpu.make_async_copy(q_ref, q_in, in_sem.at[0])
    page_in = pltpu.make_async_copy(ids_ref, ids_in, in_sem.at[1])
    query_in.start()
    page_in.start()

    barrier = pltpu.get_barrier_semaphore()

    @pl.loop(1, n)
    def _(k):
        pl.semaphore_signal(barrier, inc=1, device_id=(seg, lax.rem(me + k, n)), device_id_type=MESH)

    @pl.loop(0, half)
    def _(j):
        pl.semaphore_signal(barrier, inc=1, device_id=(behind, 2 * j + core), device_id_type=MESH)

    here = pl.ds(pl.multiple_of(core * tokens, tokens), tokens)
    key_local = pltpu.make_async_copy(key_ref, k_buf.at[here], kv_sem.at[0])
    value_local = pltpu.make_async_copy(value_ref, v_buf.at[here], kv_sem.at[1])
    key_local.start()
    value_local.start()

    @pl.loop(0, CHUNKS)
    def _(k):
        weight_copy(k).start()

    query_in.wait()
    page_in.wait()

    for c in range(2):
        for h in range(kv_heads):
            for u in range(per_kv // hpd):
                for i in range(hpd):
                    head = h * group + u * 2 * hpd + c * hpd + i
                    place = h * per_kv + u * hpd + i
                    q32[c, place:place + 1, :] = q_in[0:1, head * hd:(head + 1) * hd].astype(jnp.float32)
    q_stage[...] = q32[...].astype(jnp.bfloat16)

    head_of_lane = lax.broadcasted_iota(jnp.int32, (kv_heads, LANES), 1) // span
    pick = (head_of_lane == lax.broadcasted_iota(jnp.int32, (kv_heads, LANES), 0)).astype(jnp.float32)
    ids = ids_in[0].astype(jnp.float32)
    spread = lax.dot_general(ids, pick, (((0,), (0,)), ((), ())),
                             precision=lax.Precision.HIGHEST, preferred_element_type=jnp.float32)
    in_span = lax.rem(lax.broadcasted_iota(jnp.int32, (chosen, LANES), 1), span).astype(jnp.float32)
    offset = spread - in_span
    for j in range(half):
        hit = (jnp.abs(offset - float(j * span)) < 0.5).astype(jnp.float32)
        m_stage[j] = jnp.max(hit, axis=0, keepdims=True)

    q_buf[slot] = q_stage[core]
    m_buf[slot] = m_stage[pair]

    pl.semaphore_wait(barrier, n - 1 + half)

    def query_copy(k):
        peer = lax.rem(me + k, n)
        return pltpu.make_async_remote_copy(
            src_ref=q_stage.at[lax.rem(peer, 2)], dst_ref=q_buf.at[slot],
            send_sem=q_ssem.at[k], recv_sem=q_rsem.at[slot],
            device_id=(seg, peer), device_id_type=MESH)

    def mask_copy(k):
        peer = lax.rem(me + k, n)
        return pltpu.make_async_remote_copy(
            src_ref=m_stage.at[peer // 2], dst_ref=m_buf.at[slot],
            send_sem=m_ssem.at[k], recv_sem=m_rsem.at[slot],
            device_id=(seg, peer), device_id_type=MESH)

    @pl.loop(1, n)
    def _(k):
        query_copy(k).start()
        mask_copy(k).start()

    key_local.wait()
    value_local.wait()
    key_remote = pltpu.make_async_remote_copy(
        src_ref=k_buf.at[here], dst_ref=k_buf.at[here], send_sem=kv_send.at[0], recv_sem=kv_recv.at[0],
        device_id=(seg, mate), device_id_type=MESH)
    value_remote = pltpu.make_async_remote_copy(
        src_ref=v_buf.at[here], dst_ref=v_buf.at[here], send_sem=kv_send.at[1], recv_sem=kv_recv.at[1],
        device_id=(seg, mate), device_id_type=MESH)
    key_remote.start()
    value_remote.start()

    lane_page = lax.rem(lax.broadcasted_iota(jnp.int32, (8, LANES), 1), span)[0:1]
    token_page = lax.broadcasted_iota(jnp.int32, (2 * tokens, LANES), 0) // page
    page_hot[...] = jnp.where(lane_page == token_page, BIG, 0.0).astype(jnp.bfloat16)

    key_remote.wait()
    value_remote.wait()

    @pl.loop(1, n)
    def _(k):
        source = lax.rem(me + n - k, n)
        place = lax.rem(source, 2) * half + source // 2
        pltpu.make_async_copy(q_buf.at[place], q_buf.at[place], q_rsem.at[place]).wait()
        pltpu.make_async_copy(m_buf.at[place], m_buf.at[place], m_rsem.at[place]).wait()

    lane3 = lax.broadcasted_iota(jnp.int32, (n, 1, LANES), 2) // span
    absent = m_buf[...] - 1.0
    all_q = q_buf[...].astype(jnp.float32)
    for h in range(kv_heads):
        bias = jnp.where(lane3 == h, absent, 0.0)
        bias = jnp.broadcast_to(bias, (n, per_kv, LANES)).reshape(n * per_kv, LANES)
        q_aug[h, :, 0:hd] = all_q[:, h * per_kv:(h + 1) * per_kv, :].reshape(n * per_kv, hd).astype(jnp.bfloat16)
        q_aug[h, :, hd:hd + LANES] = bias.astype(jnp.bfloat16)

    def part_copy(j):
        return pltpu.make_async_remote_copy(
            src_ref=p_send.at[j], dst_ref=p_recv.at[pair],
            send_sem=p_ssem.at[j], recv_sem=p_rsem.at[pair],
            device_id=(seg, 2 * j + core), device_id_type=MESH)

    scale = math.log2(math.e) / math.sqrt(hd)
    lane = lax.broadcasted_iota(jnp.int32, (16, LANES), 1)
    units = per_kv // hpd

    @pl.loop(0, kv_heads)
    def _(h):
        keys = jnp.concatenate([k_buf[...], page_hot[...]], axis=1)
        values = jnp.concatenate([v_buf[...], jnp.ones((2 * tokens, LANES), jnp.bfloat16)], axis=1)
        for rb in range(n // 16):
            queries = q_aug[h, rb * 16 * per_kv:(rb + 1) * 16 * per_kv, :]
            scores = lax.dot_general(queries, keys, (((1,), (1,)), ((), ())),
                                     preferred_element_type=jnp.float32)
            top = jnp.max(scores, axis=1, keepdims=True) * scale
            weights = jnp.exp2(scores * scale - top).astype(jnp.bfloat16)
            sums = jnp.dot(weights, values, preferred_element_type=jnp.float32)
            o_scr[0] = sums[:, 0:hd] / sums[:, hd:]
            o_scr[1] = top + jnp.log2(sums[:, hd:])
            rows = slice(rb * 16, (rb + 1) * 16)
            for u in range(units):
                level = jnp.zeros((16, LANES), jnp.float32)
                for i in range(hpd):
                    index = u * hpd + i
                    value = o_scr[0, pl.ds(index, 16, stride=per_kv), :]
                    p_send[h * units + u, rows, i * hd:(i + 1) * hd] = value.astype(jnp.bfloat16)
                    level = jnp.where(lax.rem(lane, 32) == i, o_scr[1, pl.ds(index, 16, stride=per_kv), :], level)
                high = level.astype(jnp.bfloat16)
                rest = level - high.astype(jnp.float32)
                middle = rest.astype(jnp.bfloat16)
                low = rest - middle.astype(jnp.float32)
                packed = jnp.where(lane < 32, high.astype(jnp.float32),
                                   jnp.where(lane < 64, middle.astype(jnp.float32), low))
                p_send[h * units + u, rows, hpd * hd:hpd * hd + LANES] = packed.astype(jnp.bfloat16)
        for u in range(units):
            j = h * units + u

            @pl.when(j != pair)
            def _():
                part_copy(j).start()

            @pl.when(j == pair)
            def _():
                p_recv[pair] = p_send[j]

    @pl.loop(1, n)
    def _(k):
        query_copy(k).wait_send()
        mask_copy(k).wait_send()

    @pl.loop(1, half)
    def _(k):
        source = lax.rem(pair + half - k, half)
        pltpu.make_async_copy(p_recv.at[source], p_recv.at[source], p_rsem.at[source]).wait()

    levels = []
    for j in range(half):
        packed = p_recv[j, :, hpd * hd:hpd * hd + LANES].astype(jnp.float32)
        levels.append(packed + pltpu.roll(packed, 96, 1) + pltpu.roll(packed, 64, 1))
    peak = functools.reduce(jnp.maximum, levels)
    factors = [jnp.exp2(level - peak) for level in levels]
    inverse = 1.0 / functools.reduce(jnp.add, factors)
    for i in range(hpd):
        total = jnp.zeros((n, hd), jnp.float32)
        for j in range(half):
            total += factors[j][:, i:i + 1] * p_recv[j, :, i * hd:(i + 1) * hd].astype(jnp.float32)
        att[:, i * hd:(i + 1) * hd] = (total * inverse[:, i:i + 1]).astype(jnp.bfloat16)

    def core_copy(k):
        return pltpu.make_async_remote_copy(
            src_ref=c_send.at[k], dst_ref=c_recv.at[k], send_sem=c_ssem.at[k], recv_sem=c_rsem.at[k],
            device_id=(seg, mate), device_id_type=MESH)

    def final_copy(j, k):
        return pltpu.make_async_remote_copy(
            src_ref=f_send.at[k, j], dst_ref=f_recv.at[k, pair],
            send_sem=f_ssem.at[k, j], recv_sem=f_rsem.at[k, pair],
            device_id=(ahead, 2 * j + core), device_id_type=MESH)

    @pl.loop(0, CHUNKS + 1)
    def _(step):
        @pl.when(step < CHUNKS)
        def _():
            weight_copy(step).wait()
            product = jnp.dot(att[...], w_buf[step], preferred_element_type=jnp.float32)
            own_sum[step, 0] = product[0:half]
            own_sum[step, 1] = product[half:n]
            other = own_sum[step, 1 - core]
            c_send[step] = jnp.concatenate(
                [other[:, 0:cols // 2], other[:, cols // 2:]], axis=0).astype(jnp.bfloat16)
            core_copy(step).start()

        @pl.when(step > 0)
        def _():
            k = step - 1
            core_copy(k).wait_recv()
            theirs = c_recv[k].astype(jnp.float32)
            both = own_sum[k, core] + jnp.concatenate([theirs[0:half], theirs[half:n]], axis=1)
            for b in range(blocks):
                t_scr[b * half:(b + 1) * half, :] = both[:, b * LANES:(b + 1) * LANES]
            for j in range(half):
                f_send[k, j] = t_scr[pl.ds(j, blocks, stride=half), :].astype(jnp.bfloat16)

            @pl.loop(0, half)
            def _(j):
                final_copy(lax.rem(pair + j, half), k).start()

    @pl.loop(1, half)
    def _(k):
        part_copy(lax.rem(pair + k, half)).wait_send()

    @pl.loop(0, CHUNKS)
    def _(k):
        core_copy(k).wait_send()

    @pl.loop(0, CHUNKS)
    def _(k):
        @pl.loop(0, half)
        def _(j):
            pltpu.make_async_copy(f_recv.at[k, j], f_recv.at[k, j], f_rsem.at[k, j]).wait()

        total = f_recv[k, 0].astype(jnp.float32)
        for j in range(1, half):
            total += f_recv[k, j].astype(jnp.float32)
        out_ref[k] = total.astype(jnp.bfloat16)

    @pl.loop(0, CHUNKS)
    def _(k):
        @pl.loop(0, half)
        def _(j):
            final_copy(j, k).wait_send()


def local(queries, page_ids, key_pages, value_pages, out_weight):
    n = lax.axis_size("dev")
    segments = lax.axis_size("segment")
    kv_heads, chosen = page_ids.shape[1:]
    pool, page, hd = key_pages.shape
    group = queries.shape[1] // (kv_heads * hd)
    depth, width = out_weight.shape
    half = n // 2
    hpd = kv_heads * group // n
    per_kv = group // 2
    tokens = pool * page
    cols = width // CHUNKS
    blocks = cols // LANES
    dims = (n, segments, kv_heads, chosen, pool, page, hd, group, width)
    bf16, f32 = jnp.bfloat16, jnp.float32
    dma = pltpu.SemaphoreType.DMA
    vmem = pltpu.VMEM
    out = pl.pallas_call(
        functools.partial(kernel, dims),
        out_shape=jax.ShapeDtypeStruct((CHUNKS, blocks, LANES), bf16),
        in_specs=[pl.BlockSpec(memory_space=pl.ANY)] * 5,
        out_specs=pl.BlockSpec(memory_space=pltpu.VMEM),
        scratch_shapes=[
            vmem(queries.shape, bf16),
            vmem(page_ids.shape, jnp.int32),
            vmem((CHUNKS, depth, cols), bf16),
            vmem((2 * tokens, hd), bf16),
            vmem((2 * tokens, hd), bf16),
            vmem((2 * tokens, LANES), bf16),
            vmem((2, kv_heads * per_kv, hd), bf16),
            vmem((2, kv_heads * per_kv, hd), f32),
            vmem((half, 1, LANES), f32),
            vmem((n, kv_heads * per_kv, hd), bf16),
            vmem((n, 1, LANES), f32),
            vmem((kv_heads, n * per_kv, hd + LANES), bf16),
            vmem((2, 16 * per_kv, LANES), f32),
            vmem((half, n, hpd * hd + LANES), bf16),
            vmem((half, n, hpd * hd + LANES), bf16),
            vmem((n, hpd * hd), bf16),
            vmem((CHUNKS, 2, half, cols), f32),
            vmem((CHUNKS, n, cols // 2), bf16),
            vmem((CHUNKS, n, cols // 2), bf16),
            vmem((blocks * half, LANES), f32),
            vmem((CHUNKS, half, blocks, LANES), bf16),
            vmem((CHUNKS, half, blocks, LANES), bf16),
            dma((2,)), dma((CHUNKS,)), dma((2,)), dma((2,)), dma((2,)),
            dma((n,)), dma((n,)), dma((n,)), dma((n,)),
            dma((half,)), dma((half,)),
            dma((CHUNKS,)), dma((CHUNKS,)),
            dma((CHUNKS, half)), dma((CHUNKS, half)),
        ],
        compiler_params=pltpu.CompilerParams(
            collective_id=0, has_side_effects=True, vmem_limit_bytes=56 * 1024 * 1024),
    )(queries, page_ids, key_pages.reshape(tokens, hd), value_pages.reshape(tokens, hd), out_weight)
    return out.reshape(1, width)


def solution(mesh):
    placed = (
        P(("segment", "dev"), None),
        P(("segment", "dev"), None, None),
        P(("segment", "dev"), None, None),
        P(("segment", "dev"), None, None),
        P(("segment", "dev"), None),
    )
    return jax.shard_map(
        local, mesh=mesh, in_specs=placed, out_specs=P(("segment", "dev"), None), check_vma=False
    )
```

```python
import functools
import math

import jax
import jax.numpy as jnp
from jax import lax
from jax.experimental import pallas as pl
from jax.experimental.pallas import tpu as pltpu
from jax.sharding import PartitionSpec as P

MESH = pl.DeviceIdType.MESH
LANES = 128
CHUNKS = 4
BIG = float(2.0**100)


def kernel(dims, q_ref, ids_ref, key_ref, value_ref, weight_ref, out_ref,
           q_in, ids_in, w_buf, k_buf, v_buf, page_hot, q_stage, q32, m_stage, q_buf, m_buf, q_aug, o_scr,
           p_send, p_recv, att, own_sum, c_send, c_recv, t_scr, f_send, f_recv,
           in_sem, w_sem, kv_sem, kv_send, kv_recv, q_ssem, q_rsem, m_ssem, m_rsem, p_ssem, p_rsem,
           c_ssem, c_rsem, f_ssem, f_rsem):
    n, segments, kv_heads, chosen, pool, page, hd, group, width = dims
    half = n // 2
    hpd = kv_heads * group // n
    per_kv = group // 2
    tokens = pool * page
    span = 2 * pool
    cols = width // CHUNKS
    blocks = cols // LANES
    seg = lax.axis_index("segment")
    me = lax.axis_index("dev")
    core = lax.rem(me, 2)
    pair = me // 2
    mate = me + 1 - 2 * core
    slot = core * half + pair
    ahead = lax.rem(seg + 1, segments)
    behind = lax.rem(seg + segments - 1, segments)

    def weight_copy(k):
        return pltpu.make_async_copy(
            weight_ref.at[:, pl.ds(pl.multiple_of(k * cols, cols), cols)], w_buf.at[k], w_sem.at[k])

    query_in = pltpu.make_async_copy(q_ref, q_in, in_sem.at[0])
    page_in = pltpu.make_async_copy(ids_ref, ids_in, in_sem.at[1])
    query_in.start()
    page_in.start()

    barrier = pltpu.get_barrier_semaphore()

    @pl.loop(1, n)
    def _(k):
        pl.semaphore_signal(barrier, inc=1, device_id=(seg, lax.rem(me + k, n)), device_id_type=MESH)

    @pl.loop(0, half)
    def _(j):
        pl.semaphore_signal(barrier, inc=1, device_id=(behind, 2 * j + core), device_id_type=MESH)

    here = pl.ds(pl.multiple_of(core * tokens, tokens), tokens)
    key_local = pltpu.make_async_copy(key_ref, k_buf.at[here], kv_sem.at[0])
    value_local = pltpu.make_async_copy(value_ref, v_buf.at[here], kv_sem.at[1])
    key_local.start()
    value_local.start()

    @pl.loop(0, CHUNKS)
    def _(k):
        weight_copy(k).start()

    query_in.wait()
    page_in.wait()

    for c in range(2):
        for h in range(kv_heads):
            for u in range(per_kv // hpd):
                for i in range(hpd):
                    head = h * group + u * 2 * hpd + c * hpd + i
                    place = h * per_kv + u * hpd + i
                    q32[c, place:place + 1, :] = q_in[0:1, head * hd:(head + 1) * hd].astype(jnp.float32)
    q_stage[...] = q32[...].astype(jnp.bfloat16)

    head_of_lane = lax.broadcasted_iota(jnp.int32, (kv_heads, LANES), 1) // span
    pick = (head_of_lane == lax.broadcasted_iota(jnp.int32, (kv_heads, LANES), 0)).astype(jnp.float32)
    ids = ids_in[0].astype(jnp.float32)
    spread = lax.dot_general(ids, pick, (((0,), (0,)), ((), ())),
                             precision=lax.Precision.HIGHEST, preferred_element_type=jnp.float32)
    in_span = lax.rem(lax.broadcasted_iota(jnp.int32, (chosen, LANES), 1), span).astype(jnp.float32)
    offset = spread - in_span
    for j in range(half):
        hit = (jnp.abs(offset - float(j * span)) < 0.5).astype(jnp.float32)
        m_stage[j] = jnp.max(hit, axis=0, keepdims=True)

    q_buf[slot] = q_stage[core]
    m_buf[slot] = m_stage[pair]

    pl.semaphore_wait(barrier, n - 1 + half)

    def query_copy(k):
        peer = lax.rem(me + k, n)
        return pltpu.make_async_remote_copy(
            src_ref=q_stage.at[lax.rem(peer, 2)], dst_ref=q_buf.at[slot],
            send_sem=q_ssem.at[k], recv_sem=q_rsem.at[slot],
            device_id=(seg, peer), device_id_type=MESH)

    def mask_copy(k):
        peer = lax.rem(me + k, n)
        return pltpu.make_async_remote_copy(
            src_ref=m_stage.at[peer // 2], dst_ref=m_buf.at[slot],
            send_sem=m_ssem.at[k], recv_sem=m_rsem.at[slot],
            device_id=(seg, peer), device_id_type=MESH)

    @pl.loop(1, n)
    def _(k):
        query_copy(k).start()
        mask_copy(k).start()

    key_local.wait()
    value_local.wait()
    key_remote = pltpu.make_async_remote_copy(
        src_ref=k_buf.at[here], dst_ref=k_buf.at[here], send_sem=kv_send.at[0], recv_sem=kv_recv.at[0],
        device_id=(seg, mate), device_id_type=MESH)
    value_remote = pltpu.make_async_remote_copy(
        src_ref=v_buf.at[here], dst_ref=v_buf.at[here], send_sem=kv_send.at[1], recv_sem=kv_recv.at[1],
        device_id=(seg, mate), device_id_type=MESH)
    key_remote.start()
    value_remote.start()

    lane_page = lax.rem(lax.broadcasted_iota(jnp.int32, (8, LANES), 1), span)[0:1]
    token_page = lax.broadcasted_iota(jnp.int32, (2 * tokens, LANES), 0) // page
    page_hot[...] = jnp.where(lane_page == token_page, BIG, 0.0).astype(jnp.bfloat16)

    key_remote.wait()
    value_remote.wait()

    @pl.loop(1, n)
    def _(k):
        source = lax.rem(me + n - k, n)
        place = lax.rem(source, 2) * half + source // 2
        pltpu.make_async_copy(q_buf.at[place], q_buf.at[place], q_rsem.at[place]).wait()
        pltpu.make_async_copy(m_buf.at[place], m_buf.at[place], m_rsem.at[place]).wait()

    lane3 = lax.broadcasted_iota(jnp.int32, (n, 1, LANES), 2) // span
    absent = m_buf[...] - 1.0
    all_q = q_buf[...].astype(jnp.float32)
    for h in range(kv_heads):
        bias = jnp.where(lane3 == h, absent, 0.0)
        bias = jnp.broadcast_to(bias, (n, per_kv, LANES)).reshape(n * per_kv, LANES)
        q_aug[h, :, 0:hd] = all_q[:, h * per_kv:(h + 1) * per_kv, :].reshape(n * per_kv, hd).astype(jnp.bfloat16)
        q_aug[h, :, hd:hd + LANES] = bias.astype(jnp.bfloat16)

    def part_copy(j):
        return pltpu.make_async_remote_copy(
            src_ref=p_send.at[j], dst_ref=p_recv.at[pair],
            send_sem=p_ssem.at[j], recv_sem=p_rsem.at[pair],
            device_id=(seg, 2 * j + core), device_id_type=MESH)

    scale = math.log2(math.e) / math.sqrt(hd)
    lane = lax.broadcasted_iota(jnp.int32, (16, LANES), 1)
    units = per_kv // hpd

    tiles = [(h, rb) for h in range(kv_heads) for rb in range(n // 16)]
    keys = jnp.concatenate([k_buf[...], page_hot[...]], axis=1)
    values = jnp.concatenate([v_buf[...], jnp.ones((2 * tokens, LANES), jnp.bfloat16)], axis=1)

    def score(h, rb):
        queries = q_aug[h, rb * 16 * per_kv:(rb + 1) * 16 * per_kv, :]
        return lax.dot_general(queries, keys, (((1,), (1,)), ((), ())), preferred_element_type=jnp.float32)

    scores = score(*tiles[0])
    for turn, (h, rb) in enumerate(tiles):
            upcoming = score(*tiles[turn + 1]) if turn + 1 < len(tiles) else None
            top = jnp.max(scores, axis=1, keepdims=True) * scale
            weights = jnp.exp2(scores * scale - top).astype(jnp.bfloat16)
            sums = jnp.dot(weights, values, preferred_element_type=jnp.float32)
            o_scr[0] = sums[:, 0:hd] / sums[:, hd:]
            o_scr[1] = top + jnp.log2(sums[:, hd:])
            rows = slice(rb * 16, (rb + 1) * 16)
            for u in range(units):
                level = jnp.zeros((16, LANES), jnp.float32)
                for i in range(hpd):
                    index = u * hpd + i
                    value = o_scr[0, pl.ds(index, 16, stride=per_kv), :]
                    p_send[h * units + u, rows, i * hd:(i + 1) * hd] = value.astype(jnp.bfloat16)
                    level = jnp.where(lax.rem(lane, 32) == i, o_scr[1, pl.ds(index, 16, stride=per_kv), :], level)
                high = level.astype(jnp.bfloat16)
                rest = level - high.astype(jnp.float32)
                middle = rest.astype(jnp.bfloat16)
                low = rest - middle.astype(jnp.float32)
                packed = jnp.where(lane < 32, high.astype(jnp.float32),
                                   jnp.where(lane < 64, middle.astype(jnp.float32), low))
                p_send[h * units + u, rows, hpd * hd:hpd * hd + LANES] = packed.astype(jnp.bfloat16)
            scores = upcoming
            if rb + 1 < n // 16:
                continue
            for u in range(units):
                j = h * units + u

                @pl.when(j != pair)
                def _(j=j):
                    part_copy(j).start()

                @pl.when(j == pair)
                def _(j=j):
                    p_recv[pair] = p_send[j]

    @pl.loop(1, n)
    def _(k):
        query_copy(k).wait_send()
        mask_copy(k).wait_send()

    @pl.loop(1, half)
    def _(k):
        source = lax.rem(pair + half - k, half)
        pltpu.make_async_copy(p_recv.at[source], p_recv.at[source], p_rsem.at[source]).wait()

    levels = []
    for j in range(half):
        packed = p_recv[j, :, hpd * hd:hpd * hd + LANES].astype(jnp.float32)
        levels.append(packed + pltpu.roll(packed, 96, 1) + pltpu.roll(packed, 64, 1))
    peak = functools.reduce(jnp.maximum, levels)
    factors = [jnp.exp2(level - peak) for level in levels]
    inverse = 1.0 / functools.reduce(jnp.add, factors)
    for i in range(hpd):
        total = jnp.zeros((n, hd), jnp.float32)
        for j in range(half):
            total += factors[j][:, i:i + 1] * p_recv[j, :, i * hd:(i + 1) * hd].astype(jnp.float32)
        att[:, i * hd:(i + 1) * hd] = (total * inverse[:, i:i + 1]).astype(jnp.bfloat16)

    def core_copy(k):
        return pltpu.make_async_remote_copy(
            src_ref=c_send.at[k], dst_ref=c_recv.at[k], send_sem=c_ssem.at[k], recv_sem=c_rsem.at[k],
            device_id=(seg, mate), device_id_type=MESH)

    def final_copy(j, k):
        return pltpu.make_async_remote_copy(
            src_ref=f_send.at[k, j], dst_ref=f_recv.at[k, pair],
            send_sem=f_ssem.at[k, j], recv_sem=f_rsem.at[k, pair],
            device_id=(ahead, 2 * j + core), device_id_type=MESH)

    @pl.loop(0, CHUNKS + 1)
    def _(step):
        @pl.when(step < CHUNKS)
        def _():
            weight_copy(step).wait()
            product = jnp.dot(att[...], w_buf[step], preferred_element_type=jnp.float32)
            own_sum[step, 0] = product[0:half]
            own_sum[step, 1] = product[half:n]
            other = own_sum[step, 1 - core]
            c_send[step] = jnp.concatenate(
                [other[:, 0:cols // 2], other[:, cols // 2:]], axis=0).astype(jnp.bfloat16)
            core_copy(step).start()

        @pl.when(step > 0)
        def _():
            k = step - 1
            core_copy(k).wait_recv()
            theirs = c_recv[k].astype(jnp.float32)
            both = own_sum[k, core] + jnp.concatenate([theirs[0:half], theirs[half:n]], axis=1)
            for b in range(blocks):
                t_scr[b * half:(b + 1) * half, :] = both[:, b * LANES:(b + 1) * LANES]
            for j in range(half):
                f_send[k, j] = t_scr[pl.ds(j, blocks, stride=half), :].astype(jnp.bfloat16)

            @pl.loop(0, half)
            def _(j):
                final_copy(lax.rem(pair + j, half), k).start()

    @pl.loop(1, half)
    def _(k):
        part_copy(lax.rem(pair + k, half)).wait_send()

    @pl.loop(0, CHUNKS)
    def _(k):
        core_copy(k).wait_send()

    @pl.loop(0, CHUNKS)
    def _(k):
        @pl.loop(0, half)
        def _(j):
            pltpu.make_async_copy(f_recv.at[k, j], f_recv.at[k, j], f_rsem.at[k, j]).wait()

        total = f_recv[k, 0].astype(jnp.float32)
        for j in range(1, half):
            total += f_recv[k, j].astype(jnp.float32)
        for b in range(blocks):
            place = pl.ds(pl.multiple_of(k * cols + b * LANES, LANES), LANES)
            out_ref[0:1, place] = total[b:b + 1].astype(jnp.bfloat16)

    @pl.loop(0, CHUNKS)
    def _(k):
        @pl.loop(0, half)
        def _(j):
            final_copy(j, k).wait_send()


def local(queries, page_ids, key_pages, value_pages, out_weight):
    n = lax.axis_size("dev")
    segments = lax.axis_size("segment")
    kv_heads, chosen = page_ids.shape[1:]
    pool, page, hd = key_pages.shape
    group = queries.shape[1] // (kv_heads * hd)
    depth, width = out_weight.shape
    half = n // 2
    hpd = kv_heads * group // n
    per_kv = group // 2
    tokens = pool * page
    cols = width // CHUNKS
    blocks = cols // LANES
    dims = (n, segments, kv_heads, chosen, pool, page, hd, group, width)
    bf16, f32 = jnp.bfloat16, jnp.float32
    dma = pltpu.SemaphoreType.DMA
    vmem = pltpu.VMEM
    return pl.pallas_call(
        functools.partial(kernel, dims),
        out_shape=jax.ShapeDtypeStruct((1, width), bf16),
        in_specs=[pl.BlockSpec(memory_space=pl.ANY)] * 5,
        out_specs=pl.BlockSpec(memory_space=pltpu.VMEM),
        scratch_shapes=[
            vmem(queries.shape, bf16),
            vmem(page_ids.shape, jnp.int32),
            vmem((CHUNKS, depth, cols), bf16),
            vmem((2 * tokens, hd), bf16),
            vmem((2 * tokens, hd), bf16),
            vmem((2 * tokens, LANES), bf16),
            vmem((2, kv_heads * per_kv, hd), bf16),
            vmem((2, kv_heads * per_kv, hd), f32),
            vmem((half, 1, LANES), f32),
            vmem((n, kv_heads * per_kv, hd), bf16),
            vmem((n, 1, LANES), f32),
            vmem((kv_heads, n * per_kv, hd + LANES), bf16),
            vmem((2, 16 * per_kv, LANES), f32),
            vmem((half, n, hpd * hd + LANES), bf16),
            vmem((half, n, hpd * hd + LANES), bf16),
            vmem((n, hpd * hd), bf16),
            vmem((CHUNKS, 2, half, cols), f32),
            vmem((CHUNKS, n, cols // 2), bf16),
            vmem((CHUNKS, n, cols // 2), bf16),
            vmem((blocks * half, LANES), f32),
            vmem((CHUNKS, half, blocks, LANES), bf16),
            vmem((CHUNKS, half, blocks, LANES), bf16),
            dma((2,)), dma((CHUNKS,)), dma((2,)), dma((2,)), dma((2,)),
            dma((n,)), dma((n,)), dma((n,)), dma((n,)),
            dma((half,)), dma((half,)),
            dma((CHUNKS,)), dma((CHUNKS,)),
            dma((CHUNKS, half)), dma((CHUNKS, half)),
        ],
        compiler_params=pltpu.CompilerParams(
            collective_id=0, has_side_effects=True, vmem_limit_bytes=56 * 1024 * 1024),
    )(queries, page_ids, key_pages.reshape(tokens, hd), value_pages.reshape(tokens, hd), out_weight)


def solution(mesh):
    placed = (
        P(("segment", "dev"), None),
        P(("segment", "dev"), None, None),
        P(("segment", "dev"), None, None),
        P(("segment", "dev"), None, None),
        P(("segment", "dev"), None),
    )
    return jax.shard_map(
        local, mesh=mesh, in_specs=placed, out_specs=P(("segment", "dev"), None), check_vma=False
    )
```
